32 devices in a mesh: lat: 2 (over x), lon: 4 (over z), lev: 4 (over y, core).
Axes of the slice: x: 2, y: 2, z: 4, core: 2. Of those that a mesh axis runs over, the one named last changes fastest.
Arguments:
- fields: float32 [3, 16, 1280, 3072], P(None, 'lev', 'lat', 'lon'), may hold values from -6 to 6
- sl_weights: float32 [40, 24, 128, 128], P('lat', 'lon'), may hold values from -0.5 to 0.5
- sl_tile: int32 [40, 24], P('lat', 'lon'), may hold values from -1 to 1
- daylit: int32 [1280, 24], P('lat', 'lon'), may hold values from 0 to 1, as said below
- absorption: float32 [32], replicated, may hold values from 0.05 to 5
- continuum: float32 [32], replicated, may hold values from 0.05 to 2
- albedo: float32 [32], replicated, may hold values from 0.5 to 0.95
- wave_ids: int32 [640], replicated, may hold values from 0 to 639, each once
- legendre: float32 [640, 640, 1280], P(('lat', 'lon'), 'lev'), may hold values from -0.15625 to 0.15625
Outputs:
- spectral: float32 [640, 2, 3, 16, 640], P(('lat', 'lon'), None, None, None, 'lev')
The draws below stay inside these ranges and needn't reach their ends.
Inputs may be any that keep to these rules, and one draw needn't show every extreme that they name: `daylit`: in every latitude row, at most one of the blocks b and b + 12 is sunlit. `wave_ids`: every wavenumber appears in exactly one slot.
All inputs are finite; a program needn't handle non-finite values.
Results may differ from the reference program's by a relative error of at most 0.000068.
Values sent between devices are 32-bit elements; how exact they have to be, the bound alone decides.
A program may use at most 320 MiB of HBM per device.

```python
import math
import jax
import jax.numpy as jnp
from jax import lax

NLAT = 1280
NLON = 3072
MW = 640
F = 3
G = 32
TILE = 128
LATB = 32
LEV = 16


def draw_daylit(key, part):
    key_start, key_tilt, polar_key = jax.random.split(key, 3)
    segment_count = NLON // TILE
    row_ids = jnp.arange(NLAT, dtype=jnp.int32)
    sun_start = jax.random.randint(key_start, (), 0, segment_count)
    tilt_steps = jax.random.randint(key_tilt, (), 0, 4)
    polar_rows = jax.random.randint(polar_key, (), 0, NLAT // 8 + 1)
    sun_block = (sun_start + row_ids * tilt_steps * segment_count // (4 * NLAT)) % segment_count
    block_ids = jnp.arange(segment_count, dtype=jnp.int32)
    sunny = (block_ids[None, :] - sun_block[:, None]) % segment_count < segment_count // 2
    sunny = sunny & (row_ids[:, None] >= polar_rows)
    return sunny.astype(jnp.int32)


def place_ends(values, rng, low, top_value):
    shape = values.shape
    place = [jax.random.randint(jax.random.fold_in(rng, axis), (), 0, shape[axis]) for axis in range(len(shape))]
    values = values.at[tuple(place)].set(low)
    longest = shape.index(max(shape))
    place[longest] = (place[longest] + 1) % shape[longest]
    return values.at[tuple(place)].set(top_value)


def shard_levels(key, dims, cuts, smallest, top_value):
    factor_of = 1.0
    for position, shards_of in cuts:
        steps = jax.random.uniform(jax.random.fold_in(jax.random.fold_in(key, 6), position), (shards_of,), jnp.float32, smallest / len(cuts), top_value / len(cuts))
        factor_of = factor_of * jnp.repeat(jnp.exp(steps), dims[position] // shards_of).reshape((-1,) + (1,) * (len(dims) - 1 - position))
    return factor_of


def scatter_about(stream_key, dims, scale, reach, shards=(), held_as=jnp.bfloat16):
    result = scale * jax.random.normal(stream_key, dims, jnp.float32)
    if shards:
        result = result * shard_levels(stream_key, dims, shards, -0.22, 0.18)
    return jnp.clip(result, -reach, reach).astype(held_as)


def setup_inputs(seed: int = 0) -> dict:
    key_list = jax.random.split(jax.random.key(seed), 10)
    fields = scatter_about(key_list[0], (F, LEV, NLAT, NLON), 1.0, 6.0, ((1, 4), (2, 2), (3, 4)), jnp.float32)
    sl_weights = scatter_about(key_list[1], (NLAT // LATB, NLON // TILE, TILE, TILE), TILE ** -0.5, 0.5, ((0, 2), (1, 4)), jnp.float32)
    sl_tile = place_ends(jax.random.randint(key_list[2], (NLAT // LATB, NLON // TILE), -1, 2), jax.random.fold_in(key_list[2], 1), -1, 1).astype(jnp.int32)
    daylit = draw_daylit(jax.random.fold_in(key_list[9], 71), 0)
    absorption = jnp.clip(jnp.exp(jax.random.uniform(key_list[4], (G,), jnp.float32, math.log(0.05), math.log(5.0))), 0.05, 5.0)
    continuum = jnp.clip(jnp.exp(jax.random.uniform(key_list[5], (G,), jnp.float32, math.log(0.05), math.log(2.0))), 0.05, 2.0)
    albedo = jnp.clip(jax.random.uniform(key_list[6], (G,), jnp.float32, 0.5, 0.95), 0.5, 0.95)
    wave_ids = jax.random.permutation(key_list[7], MW).astype(jnp.int32)
    legendre = scatter_about(key_list[8], (MW, MW, NLAT), NLAT ** -0.5, 0.15625, ((0, 8), (1, 4)), jnp.float32)
    return {"fields": fields, "sl_weights": sl_weights, "sl_tile": sl_tile, "daylit": daylit, "absorption": absorption, "continuum": continuum, "albedo": albedo, "wave_ids": wave_ids, "legendre": legendre}


highest = lax.Precision.HIGHEST
heat_rate = 6.0
asymmetry = 0.6

def absorbed_per_band(depth_wet, hot_extinction_thickness, above_wet, above_warm, absorb_part, continuum_part, reflectivity_share):
    gamma_one = (7.0 - reflectivity_share * (4.0 + 3.0 * asymmetry)) / 4.0
    gamma_two = -(1.0 - reflectivity_share * (4.0 - 3.0 * asymmetry)) / 4.0
    eigen_rate = jnp.sqrt(gamma_one * gamma_one - gamma_two * gamma_two)
    optical = absorb_part * depth_wet + continuum_part * hot_extinction_thickness
    beam = jnp.exp(-(absorb_part * above_wet + continuum_part * above_warm))
    decay = jnp.exp(-eigen_rate * optical)
    decay_sq = decay * decay
    denominator = eigen_rate + gamma_one + (eigen_rate - gamma_one) * decay_sq
    reflect = gamma_two * (1.0 - decay_sq) / denominator
    transmit = 2.0 * eigen_rate * decay / denominator
    return beam * (1.0 - reflect - transmit)

def reference(fields, sl_weights, sl_tile, daylit, absorption, continuum, albedo, wave_ids, legendre):
    row_blocks = NLAT // LATB
    tile_count = NLON // TILE
    tile_rows = fields.reshape(F, LEV, row_blocks, LATB, tile_count, TILE)
    source_ids = (jnp.arange(tile_count, dtype=jnp.int32)[None, :] + sl_tile) % tile_count
    onehot = (source_ids[:, :, None] == jnp.arange(tile_count, dtype=jnp.int32)[None, None, :]).astype(jnp.float32)
    sources = jnp.einsum('flbrkc,bjk->flbrjc', tile_rows, onehot, precision=highest)
    departure_estimate = jnp.einsum('flbrjc,bjtc->flbrjt', sources, sl_weights, precision=highest).reshape(F, LEV, NLAT, NLON)
    moisture = departure_estimate[2]
    thermal_state = departure_estimate[0]
    stratum_factor = 4.0 / LEV
    depth_wet = stratum_factor * (0.2 + moisture * moisture)
    hot_extinction_thickness = stratum_factor * (0.2 + thermal_state * thermal_state)
    above_wet = jnp.concatenate([jnp.zeros_like(depth_wet[:1]), jnp.cumsum(depth_wet[:-1], axis=0)], axis=0)
    above_warm = jnp.concatenate([jnp.zeros_like(hot_extinction_thickness[:1]), jnp.cumsum(hot_extinction_thickness[:-1], axis=0)], axis=0)

    def add_band(band, running):
        return running + absorbed_per_band(depth_wet, hot_extinction_thickness, above_wet, above_warm, absorption[band], continuum[band], albedo[band])
    absorbed = lax.fori_loop(0, G, add_band, jnp.zeros_like(moisture)) / G
    sunlit = jnp.repeat(daylit.astype(jnp.float32), TILE, axis=1)
    heating = absorbed * sunlit[None]
    updated = jnp.concatenate([departure_estimate[:1] + heat_rate * heating[None], departure_estimate[1:]], axis=0)
    phases = wave_ids[:, None] * jnp.arange(NLON, dtype=jnp.int32)[None, :] % NLON
    angles = phases.astype(jnp.float32) * (2.0 * math.pi / NLON)
    dft_table = (jnp.stack([jnp.cos(angles), -jnp.sin(angles)], axis=1) / math.sqrt(NLON)).reshape(2 * MW, NLON)
    fourier = jnp.einsum('wn,flpn->wflp', dft_table, updated, precision=highest).reshape(MW, 2, F, LEV, NLAT)
    spectra = jnp.einsum('mcfls,mns->mcfln', fourier, legendre, precision=highest)
    keep_mask = jnp.arange(MW, dtype=jnp.int32)[None, :] >= wave_ids[:, None]
    return jnp.where(keep_mask[:, None, None, None, :], spectra, 0.0)
```

```python
import functools
import math

import jax
import jax.numpy as jnp
from jax import lax
from jax.experimental import pallas as pl
from jax.experimental.pallas import tpu as pltpu
from jax.sharding import PartitionSpec as P

high = lax.Precision.HIGH
heat_rate = 6.0
asymmetry = 0.6


def absorbed_kernel(bands, coef, dw_ref, dm_ref, aw_ref, am_ref, out_ref):
    def rows8(i, carry):
        rows = pl.ds(pl.multiple_of(i * 8, 8), 8)
        dw, dm, aw, am = dw_ref[rows, :], dm_ref[rows, :], aw_ref[rows, :], am_ref[rows, :]
        total = jnp.zeros_like(dw)
        for g in range(bands):
            beam = jnp.exp(coef[0, g] * aw + coef[1, g] * am)
            e = jnp.exp(coef[2, g] * dw + coef[3, g] * dm)
            e2 = e * e
            denominator = coef[4, g] + coef[5, g] * e2
            numerator = coef[6, g] + coef[7, g] * e2 - coef[8, g] * e
            total = total + beam * (numerator / denominator)
        out_ref[rows, :] = total * (1.0 / bands)
        return carry

    lax.fori_loop(0, out_ref.shape[0] // 8, rows8, 0)


def absorbed_mean(depth_wet, depth_warm, above_wet, above_warm, absorption, continuum, albedo):
    g1 = (7.0 - albedo * (4.0 + 3.0 * asymmetry)) / 4.0
    g2 = -(1.0 - albedo * (4.0 - 3.0 * asymmetry)) / 4.0
    k = jnp.sqrt(g1 * g1 - g2 * g2)
    coef = jnp.stack(
        [-absorption, -continuum, -k * absorption, -k * continuum, k + g1, k - g1,
         k + g1 - g2, k - g1 + g2, 2.0 * k]
    )
    shape = depth_wet.shape
    width = shape[-1]
    count = depth_wet.size // width
    block = math.gcd(count, 64)
    flat = [x.reshape(count, width) for x in (depth_wet, depth_warm, above_wet, above_warm)]
    spec = pl.BlockSpec((block, width), lambda i: (i, 0))
    bands = absorption.shape[0]
    out = pl.pallas_call(
        functools.partial(absorbed_kernel, bands),
        grid=(count // block,),
        in_specs=[pl.BlockSpec(memory_space=pltpu.SMEM)] + [spec] * 4,
        out_specs=spec,
        out_shape=jax.ShapeDtypeStruct((count, width), jnp.float32),
        cost_estimate=pl.CostEstimate(
            flops=20 * bands * count * width, bytes_accessed=20 * count * width,
            transcendentals=3 * bands * count * width,
        ),
    )(coef, *flat)
    return out.reshape(shape)


def local(fields, sl_weights, sl_tile, daylit, absorption, continuum, albedo, wave_ids, legendre):
    lon_n = lax.axis_size("lon")
    lat_n = lax.axis_size("lat")
    lev_n = lax.axis_size("lev")
    field_n, lev_l, lat_l, lon_l = fields.shape
    width = sl_weights.shape[-1]
    tiles = lon_l // width
    blocks = sl_tile.shape[0]
    block_rows = lat_l // blocks
    rows_each = lat_l // lon_n
    half = lon_n // 2
    forward = [(i, (i + 1) % lon_n) for i in range(lon_n)]
    backward = [(t, s) for s, t in forward]
    offset = sl_tile[None, :, None, :, None]

    def whole_rows(field):
        block = fields[field]
        low = lax.ppermute(block[:, :, lon_l - width :], "lon", forward)
        high_side = lax.ppermute(block[:, :, :width], "lon", backward)
        shape = (lev_l, blocks, block_rows, tiles, width)
        left = jnp.concatenate([low, block[:, :, : lon_l - width]], axis=2).reshape(shape)
        right = jnp.concatenate([block[:, :, width:], high_side], axis=2).reshape(shape)
        sources = jnp.where(offset < 0, left, jnp.where(offset > 0, right, block.reshape(shape)))
        interp = jnp.einsum("lbrjc,bjtc->lbrjt", sources, sl_weights, precision=high)
        lines = interp.reshape(lev_l, lon_n, rows_each, lon_l).transpose(1, 0, 2, 3)
        return lax.all_to_all(lines, "lon", split_axis=0, concat_axis=0, tiled=True)

    moisture = whole_rows(2)
    thermal = whole_rows(0)
    middle = whole_rows(1)

    sun = daylit.astype(jnp.float32).reshape(lon_n, rows_each, tiles)
    sun = lax.all_to_all(sun, "lon", split_axis=0, concat_axis=0, tiled=True)
    sun = jnp.broadcast_to(sun[..., None], (lon_n, rows_each, tiles, width))
    sun = sun.reshape(lon_n, 1, rows_each, lon_l)
    sun_near, sun_far = sun[:half], sun[half:]
    factor = 4.0 / (lev_l * lev_n)

    def depth_of(state):
        lit = jnp.where(sun_near > 0.0, state[:half], state[half:])
        return factor * (0.2 + lit * lit)

    depth_wet, depth_warm = depth_of(moisture), depth_of(thermal)
    totals = jnp.stack([jnp.sum(depth_wet, axis=1), jnp.sum(depth_warm, axis=1)])
    pieces = lax.all_gather(totals, "lev")
    mine = lax.axis_index("lev")
    prefix = jnp.zeros_like(totals)
    for group in range(lev_n - 1):
        prefix = prefix + jnp.where(group < mine, pieces[group], 0.0)

    def above_of(start, depth):
        levels = []
        for level in range(lev_l):
            levels.append(start)
            start = start + depth[:, level]
        return jnp.stack(levels, axis=1)

    absorbed = absorbed_mean(
        depth_wet, depth_warm, above_of(prefix[0], depth_wet), above_of(prefix[1], depth_warm),
        absorption, continuum, albedo,
    )
    heated = thermal + heat_rate * jnp.concatenate([absorbed * sun_near, absorbed * sun_far])

    lon_total = lon_l * lon_n
    wave_total = wave_ids.shape[0]
    phases = wave_ids[:, None] * jnp.arange(lon_total, dtype=jnp.int32)[None, :] % lon_total
    angles = phases.astype(jnp.float32) * (2.0 * math.pi / lon_total)
    table = jnp.stack([jnp.cos(angles), -jnp.sin(angles)], axis=1) / math.sqrt(lon_total)
    table = table.reshape(2 * wave_total, lon_total)
    waves_l = wave_total // (lat_n * lon_n)
    degree_l = legendre.shape[1]

    def spectra_of(state):
        lines = state.transpose(1, 2, 0, 3).reshape(lev_l * rows_each, lon_total)
        fourier = jnp.einsum("wn,xn->wx", table, lines, precision=high)
        out = fourier.reshape(lat_n, lon_n, 2 * waves_l, lev_l * rows_each)
        out = lax.all_to_all(out, "lat", split_axis=0, concat_axis=0, tiled=True)
        out = lax.all_to_all(out, "lon", split_axis=1, concat_axis=1, tiled=True)
        out = out.reshape(lat_n * lon_n, waves_l, 2 * lev_l, rows_each)
        out = out.transpose(1, 2, 0, 3).reshape(waves_l, 2 * lev_l, lat_n * lat_l)
        out = lax.all_gather(out, "lev")
        return jnp.einsum("Lmxs,mns->mLxn", out, legendre, precision=high)

    parts = [spectra_of(state) for state in (middle, moisture, heated)]
    spectra = jnp.stack([parts[2], parts[0], parts[1]], axis=1)
    spectra = spectra.reshape(waves_l, field_n, lev_n, 2, lev_l, degree_l)
    spectra = spectra.transpose(0, 3, 1, 2, 4, 5)
    spectra = spectra.reshape(waves_l, 2, field_n, lev_n * lev_l, degree_l)
    degrees = lax.axis_index("lev") * degree_l + jnp.arange(degree_l, dtype=jnp.int32)
    own_waves = lax.dynamic_slice_in_dim(
        wave_ids, lax.axis_index(("lat", "lon")) * waves_l, waves_l
    )
    keep_mask = degrees[None, :] >= own_waves[:, None]
    return jnp.where(keep_mask[:, None, None, None, :], spectra, 0.0)


def solution(mesh):
    in_specs = (
        P(None, "lev", "lat", "lon"),
        P("lat", "lon", None, None),
        P("lat", "lon"),
        P("lat", "lon"),
        P(),
        P(),
        P(),
        P(),
        P(("lat", "lon"), "lev", None),
    )
    out_specs = P(("lat", "lon"), None, None, None, "lev")
    return jax.shard_map(local, mesh=mesh, in_specs=in_specs, out_specs=out_specs, check_vma=False)
```
